32 devices in a mesh: blk: 8 (over z, x), head: 4 (over y, core).
Axes of the slice: x: 2, y: 2, z: 4, core: 2. Of those that a mesh axis runs over, the one named last changes fastest.
Arguments:
- queries: bfloat16 [4096, 4096], P(('blk', 'head')), may hold values from -6 to 6
- keys: bfloat16 [4096, 512], P(('blk', 'head')), may hold values from -6 to 6
- values: bfloat16 [4096, 512], P(('blk', 'head')), may hold values from -12 to 12
- vertical: int32 [32, 8, 2], replicated, may hold values from -1 to 3, as said below
- near: int32 [32, 32], P(None, 'blk'), may hold values from -1 to 2, as said below
Outputs:
- attended: bfloat16 [4096, 4096], P(('blk', 'head'))
The draws below stay inside these ranges and needn't reach their ends.
Inputs may be any that keep to these rules, and one draw needn't show every extreme that they name: vertical[h, r, c] is a key block of segment r counted from the segment's first block, or -1 for none; the two slots of one head and segment differ when neither is -1. near[h, n] is -1 or a block of the same segment as block n and strictly before it, counted from the segment's first block.
All inputs are finite; a program needn't handle non-finite values.
Results may differ from the reference program's by a relative error of at most 0.0055.
Values may be sent and summed in bfloat16 or wider, within the bound.
A program may use at most 64 MiB of HBM per device.

```python
import math
import jax
import jax.numpy as jnp
from jax import lax

QHEADS = 32
KVHEADS = 4
HEAD_DIM = 128
BLOCK = 128
SEGMENT = 512
SEG_BLOCKS = 4
TOKENS = 4096
QBLOCKS = 32
N_BLK = 8


def draw_queries(key, part):
    own_key = jax.random.fold_in(key, 1)
    values_q = jnp.clip(1.5 * jax.random.normal(own_key, (TOKENS, QHEADS, HEAD_DIM), jnp.float32), -6.0, 6.0)
    return values_q.reshape(TOKENS, QHEADS * HEAD_DIM).astype(jnp.bfloat16)


def draw_keys(key, part):
    own_key = jax.random.fold_in(key, 2)
    values_k = jnp.clip(1.5 * jax.random.normal(own_key, (TOKENS, KVHEADS, HEAD_DIM), jnp.float32), -6.0, 6.0)
    return values_k.reshape(TOKENS, KVHEADS * HEAD_DIM).astype(jnp.bfloat16)


def draw_vertical(key, part):
    base_key = jax.random.fold_in(key, 5)
    density_key, alive_key, first_key, offset_key = jax.random.split(base_key, 4)
    density = jax.random.randint(density_key, (QHEADS, 1, 1), 1, 9)
    alive = jax.random.randint(alive_key, (QHEADS, N_BLK, 2), 0, 8) < density
    first = jax.random.randint(first_key, (QHEADS, N_BLK, 1), 0, SEG_BLOCKS)
    offset = jax.random.randint(offset_key, (QHEADS, N_BLK, 1), 0, max(SEG_BLOCKS - 1, 1))
    second = (first + 1 + offset) % SEG_BLOCKS
    picked = jnp.concatenate([first, second], axis=2)
    return jnp.where(alive, picked, -1).astype(jnp.int32)


def draw_near(key, part):
    local = jnp.arange(QBLOCKS, dtype=jnp.int32) % SEG_BLOCKS
    drawn = jax.random.randint(jax.random.fold_in(key, 3), (QHEADS, QBLOCKS), 0, 1 << 20)
    return (drawn % (local[None, :] + 1) - 1).astype(jnp.int32)


def level_of(key, dims, cuts, least, high):
    level, own = 1.0, jax.random.fold_in(key, 6)
    for dim, blocks in cuts:
        draws = jnp.exp(jax.random.uniform(jax.random.fold_in(own, dim), (blocks,), jnp.float32, least / len(cuts), high / len(cuts)))
        level = level * jnp.repeat(draws, dims[dim] // blocks).reshape([-1 if axis == dim else 1 for axis in range(len(dims))])
    return level


def scatter_about(rng, shape, width, reach, shards=(), held_as=jnp.bfloat16):
    entries = width * jax.random.normal(rng, shape, jnp.float32)
    if shards:
        entries = entries * level_of(rng, shape, shards, -0.22, 0.18)
    return jnp.clip(entries, -reach, reach).astype(held_as)


def setup_inputs(seed: int = 0) -> dict:
    streams_of = jax.random.split(jax.random.key(seed), 6)
    queries = draw_queries(jax.random.fold_in(streams_of[5], 71), 0)
    keys = draw_keys(jax.random.fold_in(streams_of[5], 71), 0)
    values = scatter_about(streams_of[2], (TOKENS, KVHEADS * HEAD_DIM), 3.0, 12.0, ((0, 32),))
    vertical = draw_vertical(jax.random.fold_in(streams_of[5], 71), 0)
    near = draw_near(jax.random.fold_in(streams_of[5], 71), 0)
    return dict(queries=queries, keys=keys, values=values, vertical=vertical, near=near)


def reference(queries, keys, values, vertical, near):
    group_size = QHEADS // KVHEADS
    scaling = 1.0 / math.sqrt(HEAD_DIM)
    query_heads = queries.reshape(TOKENS, QHEADS, HEAD_DIM)
    key_heads = keys.reshape(TOKENS, KVHEADS, HEAD_DIM)
    value_heads = values.reshape(TOKENS, KVHEADS, HEAD_DIM)
    within = jnp.arange(BLOCK, dtype=jnp.int32)
    causal = within[:, None] >= within[None, :]
    segment_ids = jnp.arange(N_BLK, dtype=jnp.int32)
    lanes = jnp.arange(SEG_BLOCKS, dtype=jnp.int32)
    slot_ids = jnp.arange(2 + 2 * N_BLK, dtype=jnp.int32)

    def one_head(head_id):
        kv_id = head_id // group_size
        query_rows = lax.dynamic_index_in_dim(query_heads, head_id, 1, keepdims=False)
        key_blocks = lax.dynamic_index_in_dim(key_heads, kv_id, 1, keepdims=False).reshape(QBLOCKS, BLOCK, HEAD_DIM)
        value_blocks = lax.dynamic_index_in_dim(value_heads, kv_id, 1, keepdims=False).reshape(QBLOCKS, BLOCK, HEAD_DIM)
        vertical_rows = lax.dynamic_index_in_dim(vertical, head_id, 0, keepdims=False)
        near_rows = lax.dynamic_index_in_dim(near, head_id, 0, keepdims=False)

        def one_segment(segment_id):
            start_row = (segment_id * SEGMENT).astype(jnp.int32)
            query_tiles = lax.dynamic_slice_in_dim(query_rows, start_row, SEGMENT, 0).reshape(SEG_BLOCKS, BLOCK, HEAD_DIM)
            first_block = (segment_id * SEG_BLOCKS).astype(jnp.int32)
            near_local = lax.dynamic_slice_in_dim(near_rows, first_block, SEG_BLOCKS, 0)
            far_index = (segment_ids[:, None] * SEG_BLOCKS + jnp.maximum(vertical_rows, 0)).reshape(2 * N_BLK)
            far_live = ((vertical_rows >= 0) & (segment_ids[:, None] < segment_id)).reshape(2 * N_BLK)
            block_index = jnp.concatenate([(first_block + lanes)[:, None], (first_block + jnp.maximum(near_local, 0))[:, None], jnp.broadcast_to(far_index[None, :], (SEG_BLOCKS, 2 * N_BLK))], axis=1).astype(jnp.int32)
            block_live = jnp.concatenate([jnp.ones((SEG_BLOCKS, 1), jnp.bool_), (near_local >= 0)[:, None], jnp.broadcast_to(far_live[None, :], (SEG_BLOCKS, 2 * N_BLK))], axis=1)
            chosen_keys = key_blocks[block_index].astype(jnp.float32)
            chosen_values = value_blocks[block_index].astype(jnp.float32)
            scores = jnp.einsum('nqd,nskd->nqsk', query_tiles.astype(jnp.float32), chosen_keys) * scaling
            visible = block_live[:, None, :, None] & ((slot_ids[None, None, :, None] > 0) | causal[None, :, None, :])
            masked = jnp.where(visible, scores, -jnp.inf)
            row_max = lax.optimization_barrier(jnp.max(masked, axis=(2, 3), keepdims=True))
            weights = jnp.where(visible, jnp.exp(masked - row_max), 0.0)
            denominator = lax.optimization_barrier(jnp.sum(weights, axis=(2, 3)))
            rounded = lax.optimization_barrier(weights.astype(jnp.bfloat16)).astype(jnp.float32)
            mixed = jnp.einsum('nqsk,nskd->nqd', rounded, chosen_values) / denominator[..., None]
            return mixed.reshape(SEGMENT, HEAD_DIM)
        return lax.map(one_segment, segment_ids).reshape(TOKENS, HEAD_DIM)
    heads_out = lax.map(one_head, jnp.arange(QHEADS, dtype=jnp.int32))
    return jnp.transpose(heads_out, (1, 0, 2)).reshape(TOKENS, QHEADS * HEAD_DIM).astype(jnp.bfloat16)
```

```python
import functools
import math

import jax
import jax.numpy as jnp
from jax import lax
from jax.experimental import pallas as pl
from jax.experimental.pallas import tpu as pltpu
from jax.sharding import PartitionSpec as P

QHEADS = 32
KVHEADS = 4
HEAD_DIM = 128
BLOCK = 128
NEG = -1e30
EXP2_SCALE = math.log2(math.e) / math.sqrt(HEAD_DIM)
MESH = pl.DeviceIdType.MESH
CONTRACT_LAST = (((1,), (1,)), ((), ()))


def scores_of(query_rows, key_rows):
    return lax.dot_general(
        query_rows, key_rows, CONTRACT_LAST, preferred_element_type=jnp.float32
    )


def kernel(
    nb, nh, q_ref, k_ref, v_ref, vert_ref, near_ref, out_ref,
    qbuf, own, far, obuf,
    kv_send, kv_recv, q_send, q_recv, z_send, z_recv, x_send, x_recv, o_send, o_recv,
):
    b = lax.axis_index("blk")
    h = lax.axis_index("head")
    hh = QHEADS // nh
    rep = nh // KVHEADS
    half = nb // 2
    width = hh * HEAD_DIM
    odd = lax.rem(b, 2)
    partner = b + 1 - 2 * odd

    def lanes(index, size):
        return pl.ds(pl.multiple_of(index * size, size), size)

    def peer(d):
        return lax.rem(h + d, nh)

    barrier = pltpu.get_barrier_semaphore()
    for d in range(1, nh):
        pl.semaphore_signal(barrier, inc=1, device_id=(b, peer(d)), device_id_type=MESH)
    pl.semaphore_signal(barrier, inc=1, device_id=(partner, h), device_id_type=MESH)

    @pl.when(b + 2 < nb)
    def _():
        pl.semaphore_signal(barrier, inc=1, device_id=(b + 2, h), device_id_type=MESH)

    @pl.when(b >= 2)
    def _():
        pl.semaphore_signal(barrier, inc=1, device_id=(b - 2, h), device_id_type=MESH)

    mine = lax.div(h, rep)
    own[0, h] = k_ref[:, lanes(mine, HEAD_DIM)]
    own[1, h] = v_ref[:, lanes(mine, HEAD_DIM)]
    qbuf[h] = q_ref[:, lanes(h, width)]

    pl.semaphore_wait(
        barrier, nh + (b + 2 < nb).astype(jnp.int32) + (b >= 2).astype(jnp.int32)
    )

    def kv_copy(d, part):
        target = peer(d)
        source = (k_ref, v_ref)[part]
        return pltpu.make_async_remote_copy(
            src_ref=source.at[:, lanes(lax.div(target, rep), HEAD_DIM)],
            dst_ref=own.at[part, h],
            send_sem=kv_send.at[part, d - 1],
            recv_sem=kv_recv.at[part, d - 1],
            device_id=(b, target),
            device_id_type=MESH,
        )

    def q_copy(d):
        target = peer(d)
        return pltpu.make_async_remote_copy(
            src_ref=q_ref.at[:, lanes(target, width)],
            dst_ref=qbuf.at[h],
            send_sem=q_send.at[d - 1],
            recv_sem=q_recv.at[d - 1],
            device_id=(b, target),
            device_id_type=MESH,
        )

    def piece(j):
        return own if j == 0 else far.at[b - 2 * j]

    def z_copy(j):
        return pltpu.make_async_remote_copy(
            src_ref=piece(j),
            dst_ref=far.at[b - 2 * j],
            send_sem=z_send.at[j],
            recv_sem=z_recv.at[j],
            device_id=(b + 2, h),
            device_id_type=MESH,
        )

    def x_copy(j):
        return pltpu.make_async_remote_copy(
            src_ref=piece(j),
            dst_ref=far.at[b - 2 * j],
            send_sem=x_send.at[j],
            recv_sem=x_recv.at[j],
            device_id=(partner, h),
            device_id_type=MESH,
        )

    def arrival(slot, sem):
        return pltpu.make_async_remote_copy(
            src_ref=far.at[slot], dst_ref=far.at[slot], send_sem=sem, recv_sem=sem,
            device_id=(partner, h), device_id_type=MESH,
        )

    for part in range(2):
        for d in range(1, nh):
            kv_copy(d, part).start()
    for d in range(1, nh):
        q_copy(d).start()
    for part in range(2):
        for d in range(1, nh):
            kv_copy(d, part).wait_recv()

    def z_sends(j):
        return jnp.logical_and(b - 2 * j >= 0, b + 2 < nb)

    def x_sends(j):
        return b - 2 * j >= 0 if j else odd == 0

    for j in range(half):
        if j:
            @pl.when(b - 2 * j >= 0)
            def _():
                arrival(b - 2 * j, z_recv.at[j - 1]).wait_recv()

        @pl.when(z_sends(j))
        def _():
            z_copy(j).start()

        @pl.when(x_sends(j))
        def _():
            x_copy(j).start()

    for d in range(1, nh):
        q_copy(d).wait_recv()
    for j in range(half):
        @pl.when(partner - 2 * j >= 0 if j else odd == 1)
        def _():
            arrival(partner - 2 * j, x_recv.at[j]).wait_recv()

    tile_blocks = min(4, nh)
    rows = tile_blocks * BLOCK
    row_id = lax.broadcasted_iota(jnp.int32, (BLOCK, 2 * BLOCK), 0)
    col_id = lax.broadcasted_iota(jnp.int32, (BLOCK, 2 * BLOCK), 1)
    causal_bias = jnp.where(jnp.logical_and(col_id < BLOCK, row_id < col_id), NEG, 0.0)
    lane_id = lax.broadcasted_iota(jnp.int32, (1, 2 * BLOCK), 1)
    wide_id = lax.broadcasted_iota(jnp.int32, (1, 4 * BLOCK), 1)

    def o_copy(g, d):
        target = peer(d)
        return pltpu.make_async_remote_copy(
            src_ref=obuf.at[g, target],
            dst_ref=out_ref.at[:, lanes(h * hh + g, HEAD_DIM)],
            send_sem=o_send.at[g, d - 1],
            recv_sem=o_recv.at[g, d - 1],
            device_id=(b, target),
            device_id_type=MESH,
        )

    def head_step(g, carry):
        head = h * hh + g
        for tile in range(nh // tile_blocks):
            tops, sums, totals, queries = [], [], [], []
            for i in range(tile_blocks):
                n = tile * tile_blocks + i
                query = qbuf[n, :, lanes(g, HEAD_DIM)]
                queries.append(query)
                listed = near_ref[head, n]
                pick = jnp.maximum(listed, 0)
                key_rows = jnp.concatenate([own[0, n], own[0, pick]], axis=0)
                value_rows = jnp.concatenate([own[1, n], own[1, pick]], axis=0)
                gone = jnp.where(listed >= 0, 0.0, NEG)
                bias = causal_bias + jnp.where(lane_id < BLOCK, 0.0, gone)
                s = scores_of(query, key_rows) + bias
                top = jnp.max(s, axis=1, keepdims=True)
                w = jnp.exp2((s - top) * EXP2_SCALE)
                tops.append(top)
                sums.append(jnp.sum(w, axis=1, keepdims=True))
                totals.append(
                    jnp.dot(w.astype(jnp.bfloat16), value_rows, preferred_element_type=jnp.float32)
                )
            query_rows = jnp.concatenate(queries, axis=0)

            def far_step(t, state):
                top, total_w, acc = state
                keys_here, values_here = [], []
                bias = jnp.zeros((1, 4 * BLOCK), jnp.float32)
                for e in range(4):
                    r = 2 * t + e // 2
                    listed = vert_ref[head, r, e % 2]
                    pick = jnp.maximum(listed, 0)
                    slot = jnp.minimum(r, b - 1)
                    keys_here.append(far[slot, 0, pick])
                    values_here.append(far[slot, 1, pick])
                    live = jnp.logical_and(listed >= 0, r < b)
                    gone = jnp.where(live, 0.0, NEG)
                    inside = jnp.logical_and(wide_id >= e * BLOCK, wide_id < (e + 1) * BLOCK)
                    bias = jnp.where(inside, gone, bias)
                s = scores_of(query_rows, jnp.concatenate(keys_here, axis=0)) + bias
                new_top = jnp.maximum(top, jnp.max(s, axis=1, keepdims=True))
                shrink = jnp.exp2((top - new_top) * EXP2_SCALE)
                w = jnp.exp2((s - new_top) * EXP2_SCALE)
                total_w = total_w * shrink + jnp.sum(w, axis=1, keepdims=True)
                acc = acc * shrink + jnp.dot(
                    w.astype(jnp.bfloat16),
                    jnp.concatenate(values_here, axis=0),
                    preferred_element_type=jnp.float32,
                )
                return new_top, total_w, acc

            state = tuple(jnp.concatenate(x, axis=0) for x in (tops, sums, totals))
            _, total_w, acc = lax.fori_loop(0, lax.div(b + 1, 2), far_step, state)
            done = (acc / total_w).astype(jnp.bfloat16)
            for i in range(tile_blocks):
                obuf[g, tile * tile_blocks + i] = done[i * BLOCK : (i + 1) * BLOCK]
        out_ref[:, lanes(head, HEAD_DIM)] = obuf[g, h]
        for d in range(1, nh):
            o_copy(g, d).start()
        return carry

    lax.fori_loop(0, hh, head_step, 0)

    def finish(g, carry):
        for d in range(1, nh):
            pltpu.make_async_remote_copy(
                src_ref=obuf.at[g, h],
                dst_ref=out_ref.at[:, lanes(lax.rem(h + nh - d, nh) * hh + g, HEAD_DIM)],
                send_sem=o_send.at[g, d - 1],
                recv_sem=o_recv.at[g, d - 1],
                device_id=(b, peer(d)),
                device_id_type=MESH,
            ).wait_recv()
            o_copy(g, d).wait_send()
        return carry

    lax.fori_loop(0, hh, finish, 0)
    for d in range(1, nh):
        kv_copy(d, 0).wait_send()
        kv_copy(d, 1).wait_send()
        q_copy(d).wait_send()
    for j in range(half):
        @pl.when(z_sends(j))
        def _():
            z_copy(j).wait_send()

        @pl.when(x_sends(j))
        def _():
            x_copy(j).wait_send()


def local(queries, keys, values, vertical, near):
    nh = lax.axis_size("head")
    nb = lax.axis_size("blk")
    hh = QHEADS // nh
    assert queries.shape[0] == BLOCK and nb % 2 == 0 and nh % KVHEADS == 0
    half = nb // 2
    dma = pltpu.SemaphoreType.DMA
    vmem = pl.BlockSpec(memory_space=pltpu.VMEM)
    smem = pl.BlockSpec(memory_space=pltpu.SMEM)
    return pl.pallas_call(
        functools.partial(kernel, nb, nh),
        out_shape=jax.ShapeDtypeStruct((BLOCK, QHEADS * HEAD_DIM), jnp.bfloat16),
        in_specs=[vmem, vmem, vmem, smem, smem],
        out_specs=vmem,
        scratch_shapes=[
            pltpu.VMEM((nh, BLOCK, hh * HEAD_DIM), jnp.bfloat16),
            pltpu.VMEM((2, nh, BLOCK, HEAD_DIM), jnp.bfloat16),
            pltpu.VMEM((nb, 2, nh, BLOCK, HEAD_DIM), jnp.bfloat16),
            pltpu.VMEM((hh, nh, BLOCK, HEAD_DIM), jnp.bfloat16),
            dma((2, nh - 1)),
            dma((2, nh - 1)),
            dma((nh - 1,)),
            dma((nh - 1,)),
            dma((half,)),
            dma((half,)),
            dma((half,)),
            dma((half,)),
            dma((hh, nh - 1)),
            dma((hh, nh - 1)),
        ],
        compiler_params=pltpu.CompilerParams(
            collective_id=0, has_side_effects=True, vmem_limit_bytes=48 * 1024 * 1024
        ),
    )(queries, keys, values, vertical, near)


def solution(mesh):
    placed = (
        P(("blk", "head"), None),
        P(("blk", "head"), None),
        P(("blk", "head"), None),
        P(),
        P(None, "blk"),
    )
    return jax.shard_map(
        local, mesh=mesh, in_specs=placed, out_specs=P(("blk", "head"), None), check_vma=False
    )
```

```python
import functools
import math

import jax
import jax.numpy as jnp
from jax import lax
from jax.experimental import pallas as pl
from jax.experimental.pallas import tpu as pltpu
from jax.sharding import PartitionSpec as P

QHEADS = 32
KVHEADS = 4
HEAD_DIM = 128
BLOCK = 128
NEG = -1e30
EXP2_SCALE = math.log2(math.e) / math.sqrt(HEAD_DIM)
MESH = pl.DeviceIdType.MESH
CONTRACT_LAST = (((1,), (1,)), ((), ()))


def scores_of(query_rows, key_rows):
    return lax.dot_general(
        query_rows, key_rows, CONTRACT_LAST, preferred_element_type=jnp.float32
    )


def kernel(nb, nh, q_ref, k_ref, v_ref, vert_ref, near_ref, out_ref, *scratch):
    half = nb // 2
    far, scratch = scratch[:half], scratch[half:]
    qbuf, own, vturn, obuf, tops, sums, accs = scratch[:7]
    kv_send, kv_recv, q_send, q_recv, z_send, z_recv, x_send, x_recv, o_send, o_recv = scratch[7:]
    b = lax.axis_index("blk")
    h = lax.axis_index("head")
    hh = QHEADS // nh
    rep = nh // KVHEADS
    width = hh * HEAD_DIM
    odd = lax.rem(b, 2)
    partner = b + 1 - 2 * odd

    def lanes(index, size):
        return pl.ds(pl.multiple_of(index * size, size), size)

    def peer(d):
        return lax.rem(h + d, nh)

    barrier = pltpu.get_barrier_semaphore()
    for d in range(1, nh):
        pl.semaphore_signal(barrier, inc=1, device_id=(b, peer(d)), device_id_type=MESH)
    pl.semaphore_signal(barrier, inc=1, device_id=(partner, h), device_id_type=MESH)

    @pl.when(b + 2 < nb)
    def _():
        pl.semaphore_signal(barrier, inc=1, device_id=(b + 2, h), device_id_type=MESH)

    @pl.when(b >= 2)
    def _():
        pl.semaphore_signal(barrier, inc=1, device_id=(b - 2, h), device_id_type=MESH)

    mine = lax.div(h, rep)
    own[0, h] = k_ref[:, lanes(mine, HEAD_DIM)]
    for kv in range(KVHEADS):
        vturn[kv] = v_ref[:, kv * HEAD_DIM : (kv + 1) * HEAD_DIM].T
    own[1, h] = vturn[mine]
    qbuf[h] = q_ref[:, lanes(h, width)]

    pl.semaphore_wait(
        barrier, nh + (b + 2 < nb).astype(jnp.int32) + (b >= 2).astype(jnp.int32)
    )

    def kv_copy(d, part):
        target = peer(d)
        kv = lax.div(target, rep)
        return pltpu.make_async_remote_copy(
            src_ref=vturn.at[kv] if part else k_ref.at[:, lanes(kv, HEAD_DIM)],
            dst_ref=own.at[part, h],
            send_sem=kv_send.at[part, d - 1],
            recv_sem=kv_recv.at[part, d - 1],
            device_id=(b, target),
            device_id_type=MESH,
        )

    def q_copy(d):
        target = peer(d)
        return pltpu.make_async_remote_copy(
            src_ref=q_ref.at[:, lanes(target, width)],
            dst_ref=qbuf.at[h],
            send_sem=q_send.at[d - 1],
            recv_sem=q_recv.at[d - 1],
            device_id=(b, target),
            device_id_type=MESH,
        )

    def piece(j):
        return own if j == 0 else far[j - 1].at[1]

    def z_copy(j):
        return pltpu.make_async_remote_copy(
            src_ref=piece(j),
            dst_ref=far[j].at[1],
            send_sem=z_send.at[j],
            recv_sem=z_recv.at[j],
            device_id=(b + 2, h),
            device_id_type=MESH,
        )

    def x_copy(j, t):
        return pltpu.make_async_remote_copy(
            src_ref=piece(j),
            dst_ref=far[t].at[0],
            send_sem=x_send.at[j],
            recv_sem=x_recv.at[t],
            device_id=(partner, h),
            device_id_type=MESH,
        )

    def z_sends(j):
        return jnp.logical_and(b - 2 * j >= 0, b + 2 < nb)

    def pass_on(j):
        if j >= half:
            return
        if j:
            @pl.when(b - 2 * j >= 0)
            def _():
                z_copy(j - 1).wait_recv()

        @pl.when(z_sends(j))
        def _():
            z_copy(j).start()

        @pl.when(jnp.logical_and(odd == 0, b - 2 * j >= 0))
        def _():
            x_copy(j, j).start()

        if j:
            @pl.when(jnp.logical_and(odd == 1, b - 2 * j >= 0))
            def _():
                x_copy(j, j - 1).start()

    for part in range(2):
        for d in range(1, nh):
            kv_copy(d, part).start()
    for d in range(1, nh):
        q_copy(d).start()
    for part in range(2):
        for d in range(1, nh):
            kv_copy(d, part).wait_recv()

    pass_on(0)
    pass_on(1)
    for d in range(1, nh):
        q_copy(d).wait_recv()

    tile_blocks = min(4, nh)
    tiles = nh // tile_blocks
    key_id = lax.broadcasted_iota(jnp.int32, (BLOCK, BLOCK), 0)
    row_id = lax.broadcasted_iota(jnp.int32, (BLOCK, BLOCK), 1)
    causal_bias = jnp.where(key_id > row_id, NEG, 0.0)

    def o_copy(g, d):
        target = peer(d)
        return pltpu.make_async_remote_copy(
            src_ref=obuf.at[g, target],
            dst_ref=out_ref.at[:, lanes(h * hh + g, HEAD_DIM)],
            send_sem=o_send.at[g, d - 1],
            recv_sem=o_recv.at[g, d - 1],
            device_id=(b, target),
            device_id_type=MESH,
        )

    def weigh(s, shift):
        return jnp.exp2((s - shift) * EXP2_SCALE)

    def column_max(s):
        return jnp.max(s, axis=0, keepdims=True)

    def column_sum(w):
        return jnp.sum(w, axis=0, keepdims=True)

    def mix(values_turned, weights):
        joined = jnp.concatenate([w.astype(jnp.bfloat16) for w in weights], axis=0)
        return jnp.dot(
            jnp.concatenate(values_turned, axis=1), joined, preferred_element_type=jnp.float32
        )

    def near_step(g, carry):
        head = h * hh + g
        for n in range(nh):
            tile, at = n // tile_blocks, n % tile_blocks * BLOCK
            query = qbuf[n, :, lanes(g, HEAD_DIM)]
            listed = near_ref[head, n]
            live = listed >= 0
            pick = jnp.maximum(listed, 0)
            s0 = scores_of(own[0, n], query) + causal_bias
            s1 = scores_of(own[0, pick], query)
            top = jnp.maximum(column_max(s0), jnp.where(live, column_max(s1), NEG))
            w0 = weigh(s0, top)
            w1 = weigh(s1, jnp.where(live, top, -NEG))
            tops[g, tile, :, at : at + BLOCK] = top
            sums[g, tile, :, at : at + BLOCK] = column_sum(w0) + column_sum(w1)
            accs[g, tile, :, at : at + BLOCK] = mix([own[1, n], own[1, pick]], [w0, w1])
        return carry

    lax.fori_loop(0, hh, near_step, 0)

    for t in range(half):
        pass_on(t + 2)

        @pl.when(b - 1 - 2 * t >= 0)
        def _(t=t):
            x_copy(t, t).wait_recv()
            slots = (0, (b - 2 - 2 * t >= 0).astype(jnp.int32))

            def far_step(i, carry):
                g, tile = lax.div(i, tiles), lax.rem(i, tiles)
                head = h * hh + g
                query_rows = jnp.concatenate(
                    [
                        qbuf[tile * tile_blocks + n, :, lanes(g, HEAD_DIM)]
                        for n in range(tile_blocks)
                    ],
                    axis=0,
                )
                lives, values_turned, scores = [], [], []
                top = tops[g, tile]
                new_top = top
                for e in range(4):
                    r = b - 1 - 2 * t - e // 2
                    listed = vert_ref[head, jnp.maximum(r, 0), e % 2]
                    pick = jnp.maximum(listed, 0)
                    slot = slots[e // 2]
                    live = jnp.logical_and(listed >= 0, r >= 0)
                    lives.append(live)
                    values_turned.append(far[t][slot, 1, pick])
                    s = scores_of(far[t][slot, 0, pick], query_rows)
                    scores.append(s)
                    new_top = jnp.maximum(new_top, jnp.where(live, column_max(s), NEG))
                shrink = weigh(top, new_top)
                total = sums[g, tile] * shrink
                weights = []
                for live, s in zip(lives, scores):
                    w = weigh(s, jnp.where(live, new_top, -NEG))
                    total = total + column_sum(w)
                    weights.append(w)
                tops[g, tile] = new_top
                sums[g, tile] = total
                accs[g, tile] = accs[g, tile] * shrink + mix(values_turned, weights)
                return carry

            lax.fori_loop(0, hh * tiles, far_step, 0)

    def last_step(g, carry):
        for tile in range(tiles):
            done = (accs[g, tile] / sums[g, tile]).astype(jnp.bfloat16)
            for n in range(tile_blocks):
                obuf[g, tile * tile_blocks + n] = done[:, n * BLOCK : (n + 1) * BLOCK].T
        out_ref[:, lanes(h * hh + g, HEAD_DIM)] = obuf[g, h]
        for d in range(1, nh):
            o_copy(g, d).start()
        return carry

    lax.fori_loop(0, hh, last_step, 0)

    def finish(g, carry):
        for d in range(1, nh):
            pltpu.make_async_remote_copy(
                src_ref=obuf.at[g, h],
                dst_ref=out_ref.at[:, lanes(lax.rem(h + nh - d, nh) * hh + g, HEAD_DIM)],
                send_sem=o_send.at[g, d - 1],
                recv_sem=o_recv.at[g, d - 1],
                device_id=(b, peer(d)),
                device_id_type=MESH,
            ).wait_recv()
            o_copy(g, d).wait_send()
        return carry

    lax.fori_loop(0, hh, finish, 0)
    for d in range(1, nh):
        kv_copy(d, 0).wait_send()
        kv_copy(d, 1).wait_send()
        q_copy(d).wait_send()
    for j in range(half):
        @pl.when(z_sends(j))
        def _():
            z_copy(j).wait_send()

        @pl.when(b - 2 * j >= (0 if j else 2 * odd * nb))
        def _():
            x_copy(j, 0).wait_send()


def local(queries, keys, values, vertical, near):
    nh = lax.axis_size("head")
    nb = lax.axis_size("blk")
    hh = QHEADS // nh
    assert queries.shape[0] == BLOCK and nb % 2 == 0 and nh % KVHEADS == 0
    half = nb // 2
    tiles = nh // min(4, nh)
    dma = pltpu.SemaphoreType.DMA
    vmem = pl.BlockSpec(memory_space=pltpu.VMEM)
    smem = pl.BlockSpec(memory_space=pltpu.SMEM)
    return pl.pallas_call(
        functools.partial(kernel, nb, nh),
        out_shape=jax.ShapeDtypeStruct((BLOCK, QHEADS * HEAD_DIM), jnp.bfloat16),
        in_specs=[vmem, vmem, vmem, smem, smem],
        out_specs=vmem,
        scratch_shapes=[pltpu.VMEM((2, 2, nh, BLOCK, HEAD_DIM), jnp.bfloat16)] * half
        + [
            pltpu.VMEM((nh, BLOCK, hh * HEAD_DIM), jnp.bfloat16),
            pltpu.VMEM((2, nh, BLOCK, HEAD_DIM), jnp.bfloat16),
            pltpu.VMEM((KVHEADS, HEAD_DIM, BLOCK), jnp.bfloat16),
            pltpu.VMEM((hh, nh, BLOCK, HEAD_DIM), jnp.bfloat16),
            pltpu.VMEM((hh, tiles, 1, nh // tiles * BLOCK), jnp.float32),
            pltpu.VMEM((hh, tiles, 1, nh // tiles * BLOCK), jnp.float32),
            pltpu.VMEM((hh, tiles, HEAD_DIM, nh // tiles * BLOCK), jnp.float32),
            dma((2, nh - 1)),
            dma((2, nh - 1)),
            dma((nh - 1,)),
            dma((nh - 1,)),
            dma((half,)),
            dma((half,)),
            dma((half,)),
            dma((half,)),
            dma((hh, nh - 1)),
            dma((hh, nh - 1)),
        ],
        compiler_params=pltpu.CompilerParams(
            collective_id=0, has_side_effects=True, vmem_limit_bytes=48 * 1024 * 1024
        ),
    )(queries, keys, values, vertical, near)


def solution(mesh):
    placed = (
        P(("blk", "head"), None),
        P(("blk", "head"), None),
        P(("blk", "head"), None),
        P(),
        P(None, "blk"),
    )
    return jax.shard_map(
        local, mesh=mesh, in_specs=placed, out_specs=P(("blk", "head"), None), check_vma=False
    )
```

```python
import functools
import math

import jax
import jax.numpy as jnp
from jax import lax
from jax.experimental import pallas as pl
from jax.experimental.pallas import tpu as pltpu
from jax.sharding import PartitionSpec as P

QHEADS = 32
KVHEADS = 4
HEAD_DIM = 128
BLOCK = 128
NEG = -1e30
EXP2_SCALE = math.log2(math.e) / math.sqrt(HEAD_DIM)
MESH = pl.DeviceIdType.MESH
CONTRACT_LAST = (((1,), (1,)), ((), ()))


def scores_of(query_rows, key_rows):
    return lax.dot_general(
        query_rows, key_rows, CONTRACT_LAST, preferred_element_type=jnp.float32
    )


def kernel(nb, nh, q_ref, k_ref, v_ref, vert_ref, near_ref, out_ref, *scratch):
    half = nb // 2
    far, scratch = scratch[:half], scratch[half:]
    qbuf, own, vturn, obuf, tops, sums, accs = scratch[:7]
    kv_send, kv_recv, q_send, q_recv, z_send, z_recv, x_send, x_recv, o_send, o_recv = scratch[7:17]
    local_sem = scratch[17]
    b = lax.axis_index("blk")
    h = lax.axis_index("head")
    hh = QHEADS // nh
    rep = nh // KVHEADS
    width = hh * HEAD_DIM
    odd = lax.rem(b, 2)
    partner = b + 1 - 2 * odd

    def lanes(index, size):
        return pl.ds(pl.multiple_of(index * size, size), size)

    def peer(d):
        return lax.rem(h + d, nh)

    barrier = pltpu.get_barrier_semaphore()
    for d in range(1, nh):
        pl.semaphore_signal(barrier, inc=1, device_id=(b, peer(d)), device_id_type=MESH)
    pl.semaphore_signal(barrier, inc=1, device_id=(partner, h), device_id_type=MESH)

    @pl.when(b + 2 < nb)
    def _():
        pl.semaphore_signal(barrier, inc=1, device_id=(b + 2, h), device_id_type=MESH)

    @pl.when(b >= 2)
    def _():
        pl.semaphore_signal(barrier, inc=1, device_id=(b - 2, h), device_id_type=MESH)

    mine = lax.div(h, rep)
    own[0, h] = k_ref[:, lanes(mine, HEAD_DIM)]
    for kv in range(KVHEADS):
        vturn[kv] = v_ref[:, kv * HEAD_DIM : (kv + 1) * HEAD_DIM].T
    own[1, h] = vturn[mine]
    own_q = pltpu.make_async_copy(q_ref.at[:, lanes(h, width)], qbuf.at[h], local_sem)
    own_q.start()

    pl.semaphore_wait(
        barrier, nh + (b + 2 < nb).astype(jnp.int32) + (b >= 2).astype(jnp.int32)
    )

    def kv_copy(d, part):
        target = peer(d)
        kv = lax.div(target, rep)
        return pltpu.make_async_remote_copy(
            src_ref=vturn.at[kv] if part else k_ref.at[:, lanes(kv, HEAD_DIM)],
            dst_ref=own.at[part, h],
            send_sem=kv_send.at[part, d - 1],
            recv_sem=kv_recv.at[part, d - 1],
            device_id=(b, target),
            device_id_type=MESH,
        )

    def q_copy(d, c):
        target = peer(d)
        part = width // 2
        return pltpu.make_async_remote_copy(
            src_ref=q_ref.at[:, pl.ds(pl.multiple_of(target * width + c * part, part), part)],
            dst_ref=qbuf.at[h, :, pl.ds(c * part, part)],
            send_sem=q_send.at[c, d - 1],
            recv_sem=q_recv.at[c, d - 1],
            device_id=(b, target),
            device_id_type=MESH,
        )

    def piece(j, part):
        return own.at[part] if j == 0 else far[j - 1].at[1, part]

    def z_copy(j, part):
        return pltpu.make_async_remote_copy(
            src_ref=piece(j, part),
            dst_ref=far[j].at[1, part],
            send_sem=z_send.at[j, part],
            recv_sem=z_recv.at[j, part],
            device_id=(b + 2, h),
            device_id_type=MESH,
        )

    def x_copy(j, t, part):
        return pltpu.make_async_remote_copy(
            src_ref=piece(j, part),
            dst_ref=far[t].at[0, part],
            send_sem=x_send.at[j, part],
            recv_sem=x_recv.at[t, part],
            device_id=(partner, h),
            device_id_type=MESH,
        )

    def z_sends(j):
        return jnp.logical_and(b - 2 * j >= 0, b + 2 < nb)

    def pass_on(j):
        if j >= half:
            return
        for part in range(2):
            if j:
                @pl.when(b - 2 * j >= 0)
                def _():
                    z_copy(j - 1, part).wait_recv()

            @pl.when(z_sends(j))
            def _():
                z_copy(j, part).start()

            @pl.when(jnp.logical_and(odd == 0, b - 2 * j >= 0))
            def _():
                x_copy(j, j, part).start()

            if j:
                @pl.when(jnp.logical_and(odd == 1, b - 2 * j >= 0))
                def _():
                    x_copy(j, j - 1, part).start()

    for part in range(2):
        for d in range(1, nh):
            kv_copy(d, part).start()
    for part in range(2):
        for d in range(1, nh):
            kv_copy(d, part).wait_recv()
    for c in range(2):
        for d in range(1, nh):
            q_copy(d, c).start()

    pass_on(0)
    pass_on(1)
    own_q.wait()

    tile_blocks = min(4, nh)
    tiles = nh // tile_blocks
    key_id = lax.broadcasted_iota(jnp.int32, (BLOCK, BLOCK), 0)
    row_id = lax.broadcasted_iota(jnp.int32, (BLOCK, BLOCK), 1)
    causal_bias = jnp.where(key_id > row_id, NEG, 0.0)

    def o_copy(g, d):
        target = peer(d)
        return pltpu.make_async_remote_copy(
            src_ref=obuf.at[g, target],
            dst_ref=out_ref.at[:, lanes(h * hh + g, HEAD_DIM)],
            send_sem=o_send.at[g, d - 1],
            recv_sem=o_recv.at[g, d - 1],
            device_id=(b, target),
            device_id_type=MESH,
        )

    def weigh(s, shift):
        return jnp.exp2((s - shift) * EXP2_SCALE)

    def column_max(s):
        return jnp.max(s, axis=0, keepdims=True)

    def column_sum(w):
        return jnp.sum(w, axis=0, keepdims=True)

    def mix(values_turned, weights):
        joined = jnp.concatenate([w.astype(jnp.bfloat16) for w in weights], axis=0)
        return jnp.dot(
            jnp.concatenate(values_turned, axis=1), joined, preferred_element_type=jnp.float32
        )

    near_pair = min(2, hh // 2)

    def near_step(i, carry):
        results = []
        for u in range(near_pair):
            g = i * near_pair + u
            head = h * hh + g
            for n in range(nh):
                query = qbuf[n, :, lanes(g, HEAD_DIM)]
                listed = near_ref[head, n]
                live = listed >= 0
                pick = jnp.maximum(listed, 0)
                both = scores_of(jnp.concatenate([own[0, n], own[0, pick]], axis=0), query)
                s0 = both[:BLOCK] + causal_bias
                s1 = both[BLOCK:]
                top = jnp.maximum(column_max(s0), jnp.where(live, column_max(s1), NEG))
                w0 = weigh(s0, top)
                w1 = weigh(s1, jnp.where(live, top, -NEG))
                total = column_sum(w0) + column_sum(w1)
                results.append((g, n, top, total, mix([own[1, n], own[1, pick]], [w0, w1])))
        for g, n, top, total, mixed in results:
            tile, at = n // tile_blocks, n % tile_blocks * BLOCK
            tops[g, tile, :, at : at + BLOCK] = top
            sums[g, tile, :, at : at + BLOCK] = total
            accs[g, tile, :, at : at + BLOCK] = mixed
        return carry

    steps = hh // 2 // near_pair
    for c in range(2):
        for d in range(1, nh):
            q_copy(d, c).wait_recv()
        lax.fori_loop(c * steps, (c + 1) * steps, near_step, 0)
        pass_on(2 + c)

    def last_step(g, carry):
        for tile in range(tiles):
            done = (accs[g, tile] / sums[g, tile]).astype(jnp.bfloat16)
            for n in range(tile_blocks):
                obuf[g, tile * tile_blocks + n] = done[:, n * BLOCK : (n + 1) * BLOCK].T
        out_ref[:, lanes(h * hh + g, HEAD_DIM)] = obuf[g, h]
        for d in range(1, nh):
            o_copy(g, d).start()
        return carry

    for t in range(half):
        pass_on(t + 4)

        @pl.when(b - 1 - 2 * t >= 0)
        def _(t=t):
            x_copy(t, t, 0).wait_recv()
            x_copy(t, t, 1).wait_recv()
            slots = (0, (b - 2 - 2 * t >= 0).astype(jnp.int32))

            def far_step(i, carry):
                first, tile = lax.div(i, tiles) * far_pair, lax.rem(i, tiles)
                heads_now = [first + u for u in range(far_pair)]
                results = [far_tile(g, tile) for g in heads_now]
                for g, (top, total, acc) in zip(heads_now, results):
                    tops[g, tile] = top
                    sums[g, tile] = total
                    accs[g, tile] = acc

                @pl.when(jnp.logical_and(b - 3 - 2 * t < 0, tile == tiles - 1))
                def _():
                    for g in heads_now:
                        last_step(g, 0)

                return carry

            def far_tile(g, tile):
                head = h * hh + g
                query_rows = jnp.concatenate(
                    [
                        qbuf[tile * tile_blocks + n, :, lanes(g, HEAD_DIM)]
                        for n in range(tile_blocks)
                    ],
                    axis=0,
                )
                lives, keys_here, values_turned = [], [], []
                for e in range(4):
                    r = b - 1 - 2 * t - e // 2
                    listed = vert_ref[head, jnp.maximum(r, 0), e % 2]
                    pick = jnp.maximum(listed, 0)
                    slot = slots[e // 2]
                    lives.append(jnp.logical_and(listed >= 0, r >= 0))
                    keys_here.append(far[t][slot, 0, pick])
                    values_turned.append(far[t][slot, 1, pick])
                every = scores_of(jnp.concatenate(keys_here, axis=0), query_rows)
                top = tops[g, tile]
                new_top = top
                for e in range(4):
                    peak = column_max(every[e * BLOCK : (e + 1) * BLOCK])
                    new_top = jnp.maximum(new_top, jnp.where(lives[e], peak, NEG))
                shrink = weigh(top, new_top)
                total = sums[g, tile] * shrink
                weights = []
                for e in range(4):
                    w = weigh(
                        every[e * BLOCK : (e + 1) * BLOCK], jnp.where(lives[e], new_top, -NEG)
                    )
                    total = total + column_sum(w)
                    weights.append(w)
                return new_top, total, accs[g, tile] * shrink + mix(values_turned, weights)

            far_pair = min(2, hh)
            lax.fori_loop(0, hh // far_pair * tiles, far_step, 0)

    @pl.when(b == 0)
    def _():
        lax.fori_loop(0, hh, last_step, 0)

    def finish(g, carry):
        for d in range(1, nh):
            pltpu.make_async_remote_copy(
                src_ref=obuf.at[g, h],
                dst_ref=out_ref.at[:, lanes(lax.rem(h + nh - d, nh) * hh + g, HEAD_DIM)],
                send_sem=o_send.at[g, d - 1],
                recv_sem=o_recv.at[g, d - 1],
                device_id=(b, peer(d)),
                device_id_type=MESH,
            ).wait_recv()
            o_copy(g, d).wait_send()
        return carry

    lax.fori_loop(0, hh, finish, 0)
    for d in range(1, nh):
        kv_copy(d, 0).wait_send()
        kv_copy(d, 1).wait_send()
        q_copy(d, 0).wait_send()
        q_copy(d, 1).wait_send()
    for j in range(half):
        for part in range(2):
            @pl.when(z_sends(j))
            def _():
                z_copy(j, part).wait_send()

            @pl.when(b - 2 * j >= (0 if j else 2 * odd * nb))
            def _():
                x_copy(j, 0, part).wait_send()


def local(queries, keys, values, vertical, near):
    nh = lax.axis_size("head")
    nb = lax.axis_size("blk")
    hh = QHEADS // nh
    assert queries.shape[0] == BLOCK and nb % 2 == 0 and nh % KVHEADS == 0
    half = nb // 2
    tiles = nh // min(4, nh)
    dma = pltpu.SemaphoreType.DMA
    vmem = pl.BlockSpec(memory_space=pltpu.VMEM)
    smem = pl.BlockSpec(memory_space=pltpu.SMEM)
    return pl.pallas_call(
        functools.partial(kernel, nb, nh),
        out_shape=jax.ShapeDtypeStruct((BLOCK, QHEADS * HEAD_DIM), jnp.bfloat16),
        in_specs=[pl.BlockSpec(memory_space=pl.ANY), vmem, vmem, smem, smem],
        out_specs=vmem,
        scratch_shapes=[pltpu.VMEM((2, 2, nh, BLOCK, HEAD_DIM), jnp.bfloat16)] * half
        + [
            pltpu.VMEM((nh, BLOCK, hh * HEAD_DIM), jnp.bfloat16),
            pltpu.VMEM((2, nh, BLOCK, HEAD_DIM), jnp.bfloat16),
            pltpu.VMEM((KVHEADS, HEAD_DIM, BLOCK), jnp.bfloat16),
            pltpu.VMEM((hh, nh, BLOCK, HEAD_DIM), jnp.bfloat16),
            pltpu.VMEM((hh, tiles, 1, nh // tiles * BLOCK), jnp.float32),
            pltpu.VMEM((hh, tiles, 1, nh // tiles * BLOCK), jnp.float32),
            pltpu.VMEM((hh, tiles, HEAD_DIM, nh // tiles * BLOCK), jnp.float32),
            dma((2, nh - 1)),
            dma((2, nh - 1)),
            dma((2, nh - 1)),
            dma((2, nh - 1)),
            dma((half, 2)),
            dma((half, 2)),
            dma((half, 2)),
            dma((half, 2)),
            dma((hh, nh - 1)),
            dma((hh, nh - 1)),
            dma,
        ],
        compiler_params=pltpu.CompilerParams(
            collective_id=0, has_side_effects=True, vmem_limit_bytes=48 * 1024 * 1024
        ),
    )(queries, keys, values, vertical, near)


def solution(mesh):
    placed = (
        P(("blk", "head"), None),
        P(("blk", "head"), None),
        P(("blk", "head"), None),
        P(),
        P(None, "blk"),
    )
    return jax.shard_map(
        local, mesh=mesh, in_specs=placed, out_specs=P(("blk", "head"), None), check_vma=False
    )
```

```python
import functools
import math

import jax
import jax.numpy as jnp
from jax import lax
from jax.experimental import pallas as pl
from jax.experimental.pallas import tpu as pltpu
from jax.sharding import PartitionSpec as P

QHEADS = 32
KVHEADS = 4
HEAD_DIM = 128
BLOCK = 128
NEG = -1e30
EXP2_SCALE = math.log2(math.e) / math.sqrt(HEAD_DIM)
MESH = pl.DeviceIdType.MESH


def scores_of(key_rows, query_turned):
    return jnp.dot(key_rows, query_turned, preferred_element_type=jnp.float32)


def kernel(nb, nh, q_ref, k_ref, v_ref, vert_ref, near_ref, out_ref, *scratch):
    half = nb // 2
    far, scratch = scratch[:half], scratch[half:]
    qbuf, own, vturn, obuf, tops, sums, accs = scratch[:7]
    kv_send, kv_recv, q_send, q_recv, z_send, z_recv, x_send, x_recv, o_send, o_recv = scratch[7:17]
    local_sem, qrows, qturn = scratch[17:]
    b = lax.axis_index("blk")
    h = lax.axis_index("head")
    hh = QHEADS // nh
    rep = nh // KVHEADS
    odd = lax.rem(b, 2)
    partner = b + 1 - 2 * odd

    def lanes(index, size):
        return pl.ds(pl.multiple_of(index * size, size), size)

    def peer(d):
        return lax.rem(h + d, nh)

    barrier = pltpu.get_barrier_semaphore()
    for d in range(1, nh):
        pl.semaphore_signal(barrier, inc=1, device_id=(b, peer(d)), device_id_type=MESH)
    pl.semaphore_signal(barrier, inc=1, device_id=(partner, h), device_id_type=MESH)

    @pl.when(b + 2 < nb)
    def _():
        pl.semaphore_signal(barrier, inc=1, device_id=(b + 2, h), device_id_type=MESH)

    @pl.when(b >= 2)
    def _():
        pl.semaphore_signal(barrier, inc=1, device_id=(b - 2, h), device_id_type=MESH)

    mine = lax.div(h, rep)
    own[0, h] = k_ref[:, lanes(mine, HEAD_DIM)]
    for kv in range(KVHEADS):
        vturn[kv] = v_ref[:, kv * HEAD_DIM : (kv + 1) * HEAD_DIM].T
    own[1, h] = vturn[mine]
    fetch = pltpu.make_async_copy(q_ref, qrows, local_sem)
    fetch.start()

    pl.semaphore_wait(
        barrier, nh + (b + 2 < nb).astype(jnp.int32) + (b >= 2).astype(jnp.int32)
    )

    def kv_copy(d, part):
        target = peer(d)
        kv = lax.div(target, rep)
        return pltpu.make_async_remote_copy(
            src_ref=vturn.at[kv] if part else k_ref.at[:, lanes(kv, HEAD_DIM)],
            dst_ref=own.at[part, h],
            send_sem=kv_send.at[part, d - 1],
            recv_sem=kv_recv.at[part, d - 1],
            device_id=(b, target),
            device_id_type=MESH,
        )

    def q_copy(d, c):
        target = peer(d)
        count = hh // 2
        return pltpu.make_async_remote_copy(
            src_ref=qturn.at[pl.ds(target * hh + c * count, count)],
            dst_ref=qbuf.at[h, pl.ds(c * count, count)],
            send_sem=q_send.at[c, d - 1],
            recv_sem=q_recv.at[c, d - 1],
            device_id=(b, target),
            device_id_type=MESH,
        )

    def piece(j, part):
        return own.at[part] if j == 0 else far[j - 1].at[1, part]

    def z_copy(j, part):
        return pltpu.make_async_remote_copy(
            src_ref=piece(j, part),
            dst_ref=far[j].at[1, part],
            send_sem=z_send.at[j, part],
            recv_sem=z_recv.at[j, part],
            device_id=(b + 2, h),
            device_id_type=MESH,
        )

    def x_copy(j, t, part):
        return pltpu.make_async_remote_copy(
            src_ref=piece(j, part),
            dst_ref=far[t].at[0, part],
            send_sem=x_send.at[j, part],
            recv_sem=x_recv.at[t, part],
            device_id=(partner, h),
            device_id_type=MESH,
        )

    def z_sends(j):
        return jnp.logical_and(b - 2 * j >= 0, b + 2 < nb)

    def pass_on(j):
        if j >= half:
            return
        for part in range(2):
            if j:
                @pl.when(b - 2 * j >= 0)
                def _():
                    z_copy(j - 1, part).wait_recv()

            @pl.when(z_sends(j))
            def _():
                z_copy(j, part).start()

            @pl.when(jnp.logical_and(odd == 0, b - 2 * j >= 0))
            def _():
                x_copy(j, j, part).start()

            if j:
                @pl.when(jnp.logical_and(odd == 1, b - 2 * j >= 0))
                def _():
                    x_copy(j, j - 1, part).start()

    for part in range(2):
        for d in range(1, nh):
            kv_copy(d, part).start()
    fetch.wait()

    def turn_step(i, carry):
        for u in range(4):
            qturn[i * 4 + u] = qrows[:, pl.ds(pl.multiple_of((i * 4 + u) * BLOCK, BLOCK), BLOCK)].T
        return carry

    lax.fori_loop(0, QHEADS // 4, turn_step, 0)
    for g in range(hh):
        qbuf[h, g] = qturn[h * hh + g]
    for part in range(2):
        for d in range(1, nh):
            kv_copy(d, part).wait_recv()
    for c in range(2):
        for d in range(1, nh):
            q_copy(d, c).start()

    pass_on(0)
    pass_on(1)

    tile_blocks = min(4, nh)
    tiles = nh // tile_blocks
    key_id = lax.broadcasted_iota(jnp.int32, (BLOCK, BLOCK), 0)
    row_id = lax.broadcasted_iota(jnp.int32, (BLOCK, BLOCK), 1)
    causal_bias = jnp.where(key_id > row_id, NEG, 0.0)

    def o_copy(g, d):
        target = peer(d)
        return pltpu.make_async_remote_copy(
            src_ref=obuf.at[g, target],
            dst_ref=out_ref.at[:, lanes(h * hh + g, HEAD_DIM)],
            send_sem=o_send.at[g, d - 1],
            recv_sem=o_recv.at[g, d - 1],
            device_id=(b, target),
            device_id_type=MESH,
        )

    def weigh(s, shift):
        return jnp.exp2((s - shift) * EXP2_SCALE)

    def column_max(s):
        return jnp.max(s, axis=0, keepdims=True)

    def column_sum(w):
        return jnp.sum(w, axis=0, keepdims=True)

    def mix(values_turned, weights):
        joined = jnp.concatenate([w.astype(jnp.bfloat16) for w in weights], axis=0)
        return jnp.dot(
            jnp.concatenate(values_turned, axis=1), joined, preferred_element_type=jnp.float32
        )

    near_pair = min(2, hh // 2)

    def near_step(i, carry):
        results = []
        for u in range(near_pair):
            g = i * near_pair + u
            head = h * hh + g
            for n in range(nh):
                query = qbuf[n, g]
                listed = near_ref[head, n]
                live = listed >= 0
                pick = jnp.maximum(listed, 0)
                both = scores_of(jnp.concatenate([own[0, n], own[0, pick]], axis=0), query)
                s0 = both[:BLOCK] + causal_bias
                s1 = both[BLOCK:]
                top = jnp.maximum(column_max(s0), jnp.where(live, column_max(s1), NEG))
                w0 = weigh(s0, top)
                w1 = weigh(s1, jnp.where(live, top, -NEG))
                total = column_sum(w0) + column_sum(w1)
                results.append((g, n, top, total, mix([own[1, n], own[1, pick]], [w0, w1])))
        for g, n, top, total, mixed in results:
            tile, at = n // tile_blocks, n % tile_blocks * BLOCK
            tops[g, tile, :, at : at + BLOCK] = top
            sums[g, tile, :, at : at + BLOCK] = total
            accs[g, tile, :, at : at + BLOCK] = mixed
        return carry

    steps = hh // 2 // near_pair
    for c in range(2):
        for d in range(1, nh):
            q_copy(d, c).wait_recv()
        lax.fori_loop(c * steps, (c + 1) * steps, near_step, 0)
        pass_on(2 + c)

    def last_step(g, carry):
        for tile in range(tiles):
            done = (accs[g, tile] / sums[g, tile]).astype(jnp.bfloat16)
            for n in range(tile_blocks):
                obuf[g, tile * tile_blocks + n] = done[:, n * BLOCK : (n + 1) * BLOCK].T
        out_ref[:, lanes(h * hh + g, HEAD_DIM)] = obuf[g, h]
        for d in range(1, nh):
            o_copy(g, d).start()
        return carry

    for t in range(half):
        pass_on(t + 4)

        @pl.when(b - 1 - 2 * t >= 0)
        def _(t=t):
            x_copy(t, t, 0).wait_recv()
            x_copy(t, t, 1).wait_recv()
            slots = (0, (b - 2 - 2 * t >= 0).astype(jnp.int32))

            def far_step(i, carry):
                first, tile = lax.div(i, tiles) * far_pair, lax.rem(i, tiles)
                heads_now = [first + u for u in range(far_pair)]
                results = [far_tile(g, tile) for g in heads_now]
                for g, (top, total, acc) in zip(heads_now, results):
                    tops[g, tile] = top
                    sums[g, tile] = total
                    accs[g, tile] = acc

                @pl.when(jnp.logical_and(b - 3 - 2 * t < 0, tile == tiles - 1))
                def _():
                    for g in heads_now:
                        last_step(g, 0)

                return carry

            def far_tile(g, tile):
                head = h * hh + g
                query_turned = jnp.concatenate(
                    [
                        qbuf[tile * tile_blocks + n, g]
                        for n in range(tile_blocks)
                    ],
                    axis=1,
                )
                lives, keys_here, values_turned = [], [], []
                for e in range(4):
                    r = b - 1 - 2 * t - e // 2
                    listed = vert_ref[head, jnp.maximum(r, 0), e % 2]
                    pick = jnp.maximum(listed, 0)
                    slot = slots[e // 2]
                    lives.append(jnp.logical_and(listed >= 0, r >= 0))
                    keys_here.append(far[t][slot, 0, pick])
                    values_turned.append(far[t][slot, 1, pick])
                every = scores_of(jnp.concatenate(keys_here, axis=0), query_turned)
                top = tops[g, tile]
                new_top = top
                for e in range(4):
                    peak = column_max(every[e * BLOCK : (e + 1) * BLOCK])
                    new_top = jnp.maximum(new_top, jnp.where(lives[e], peak, NEG))
                shrink = weigh(top, new_top)
                total = sums[g, tile] * shrink
                weights = []
                for e in range(4):
                    w = weigh(
                        every[e * BLOCK : (e + 1) * BLOCK], jnp.where(lives[e], new_top, -NEG)
                    )
                    total = total + column_sum(w)
                    weights.append(w)
                return new_top, total, accs[g, tile] * shrink + mix(values_turned, weights)

            far_pair = min(2, hh)
            lax.fori_loop(0, hh // far_pair * tiles, far_step, 0)

    @pl.when(b == 0)
    def _():
        lax.fori_loop(0, hh, last_step, 0)

    def finish(g, carry):
        for d in range(1, nh):
            pltpu.make_async_remote_copy(
                src_ref=obuf.at[g, h],
                dst_ref=out_ref.at[:, lanes(lax.rem(h + nh - d, nh) * hh + g, HEAD_DIM)],
                send_sem=o_send.at[g, d - 1],
                recv_sem=o_recv.at[g, d - 1],
                device_id=(b, peer(d)),
                device_id_type=MESH,
            ).wait_recv()
            o_copy(g, d).wait_send()
        return carry

    lax.fori_loop(0, hh, finish, 0)
    for d in range(1, nh):
        kv_copy(d, 0).wait_send()
        kv_copy(d, 1).wait_send()
        q_copy(d, 0).wait_send()
        q_copy(d, 1).wait_send()
    for j in range(half):
        for part in range(2):
            @pl.when(z_sends(j))
            def _():
                z_copy(j, part).wait_send()

            @pl.when(b - 2 * j >= (0 if j else 2 * odd * nb))
            def _():
                x_copy(j, 0, part).wait_send()


def local(queries, keys, values, vertical, near):
    nh = lax.axis_size("head")
    nb = lax.axis_size("blk")
    hh = QHEADS // nh
    assert queries.shape[0] == BLOCK and nb % 2 == 0 and nh % KVHEADS == 0
    half = nb // 2
    tiles = nh // min(4, nh)
    dma = pltpu.SemaphoreType.DMA
    vmem = pl.BlockSpec(memory_space=pltpu.VMEM)
    smem = pl.BlockSpec(memory_space=pltpu.SMEM)
    return pl.pallas_call(
        functools.partial(kernel, nb, nh),
        out_shape=jax.ShapeDtypeStruct((BLOCK, QHEADS * HEAD_DIM), jnp.bfloat16),
        in_specs=[pl.BlockSpec(memory_space=pl.ANY), vmem, vmem, smem, smem],
        out_specs=vmem,
        scratch_shapes=[pltpu.VMEM((2, 2, nh, BLOCK, HEAD_DIM), jnp.bfloat16)] * half
        + [
            pltpu.VMEM((nh, hh, HEAD_DIM, BLOCK), jnp.bfloat16),
            pltpu.VMEM((2, nh, BLOCK, HEAD_DIM), jnp.bfloat16),
            pltpu.VMEM((KVHEADS, HEAD_DIM, BLOCK), jnp.bfloat16),
            pltpu.VMEM((hh, nh, BLOCK, HEAD_DIM), jnp.bfloat16),
            pltpu.VMEM((hh, tiles, 1, nh // tiles * BLOCK), jnp.float32),
            pltpu.VMEM((hh, tiles, 1, nh // tiles * BLOCK), jnp.float32),
            pltpu.VMEM((hh, tiles, HEAD_DIM, nh // tiles * BLOCK), jnp.float32),
            dma((2, nh - 1)),
            dma((2, nh - 1)),
            dma((2, nh - 1)),
            dma((2, nh - 1)),
            dma((half, 2)),
            dma((half, 2)),
            dma((half, 2)),
            dma((half, 2)),
            dma((hh, nh - 1)),
            dma((hh, nh - 1)),
            dma,
            pltpu.VMEM((BLOCK, QHEADS * HEAD_DIM), jnp.bfloat16),
            pltpu.VMEM((QHEADS, HEAD_DIM, BLOCK), jnp.bfloat16),
        ],
        compiler_params=pltpu.CompilerParams(
            collective_id=0, has_side_effects=True, vmem_limit_bytes=48 * 1024 * 1024
        ),
    )(queries, keys, values, vertical, near)


def solution(mesh):
    placed = (
        P(("blk", "head"), None),
        P(("blk", "head"), None),
        P(("blk", "head"), None),
        P(),
        P(None, "blk"),
    )
    return jax.shard_map(
        local, mesh=mesh, in_specs=placed, out_specs=P(("blk", "head"), None), check_vma=False
    )
```
